256 devices in a mesh: dp: 32 (over z, y), expert: 8 (over x, core).
Axes of the slice: x: 4, y: 4, z: 8, core: 2. Of those that a mesh axis runs over, the one named last changes fastest.
Arguments:
- grad_out: bfloat16 [131072, 4096], P(('dp', 'expert')), may hold values from -6 to 6
- expert_ids: int32 [131072, 8], P(('dp', 'expert')), may hold values from 0 to 127, as said below
- route_weights: bfloat16 [131072, 8], P(('dp', 'expert')), may hold values from 0.049804688 to 0.5
- saved_preact: bfloat16 [8, 32, 8, 64, 3072], P('expert', 'dp'), may hold values from -6 to 6
- down_weight: bfloat16 [8, 1536, 4096], P('expert', 'dp'), may hold values from -0.15625 to 0.15625
Outputs:
- route_grad: float32 [131072, 8], P(('dp', 'expert'))
- preact_grad: bfloat16 [8, 32, 8, 64, 3072], P('expert', 'dp')
- down_grad: float32 [8, 1536, 4096], P('expert', 'dp')
The draws below stay inside these ranges and needn't reach their ends.
Inputs may be any that keep to these rules, and one draw needn't show every extreme that they name: `expert_ids`: each token's 8 ids are distinct. At most 64 tokens of one device name any one expert below 8; in every data index, some expert below 8 is named by exactly 64 tokens of each of its 8 devices.
All inputs are finite; a program needn't handle non-finite values.
Results may differ from the reference program's by a relative error of at most 0.024.
Values may be sent and summed in bfloat16 or wider, within the bound.
No kernel may reach another device: no remote copies, remote signals or barrier semaphores. Data moves between devices by JAX's collectives and lax.ppermute only.
A program may use at most 128 MiB of HBM per device.

```python
import jax
import jax.numpy as jnp
from jax import lax

D = 4096
FF = 1536
EXPERTS = 128
TOP = 8
TOK_DEV = 512
CAP = 64
FLIGHT = 8
TOKENS = 131072
N_DP = 32
N_EXPERT = 8


def draw_expert_ids(key, part):
    blocks = N_DP * N_EXPERT
    keys = jax.random.split(key, 5)
    shifts = jax.random.randint(keys[0], (blocks, FLIGHT), 0, 4)
    counts = jnp.maximum(CAP // jnp.left_shift(1, shifts), 1)
    group_pick = jax.random.randint(keys[1], (N_DP,), 0, FLIGHT)
    full_one = jnp.repeat(group_pick, N_EXPERT)
    labels = jnp.arange(FLIGHT)
    counts = jnp.where(labels[None, :] == full_one[:, None], CAP, counts)
    perm_keys = jax.random.split(keys[2], blocks * FLIGHT)
    ranks = jax.vmap(lambda k: jax.random.permutation(k, TOK_DEV))(perm_keys).reshape(blocks, FLIGHT, TOK_DEV)
    member = jnp.transpose(ranks < counts[:, :, None], (0, 2, 1))
    rotate = jax.random.randint(keys[3], (blocks, TOK_DEV), 0, FLIGHT)
    slots = jnp.arange(TOP)
    flight_id = (slots[None, None, :] + rotate[:, :, None]) % FLIGHT
    used = jnp.take_along_axis(member, flight_id, axis=2) & (slots[None, None, :] < FLIGHT)
    spread = EXPERTS - FLIGHT
    stride = spread // TOP
    base = jax.random.randint(keys[4], (blocks, TOK_DEV), 0, spread)
    others = FLIGHT + (base[:, :, None] + slots[None, None, :] * stride) % spread
    result = jnp.where(used, flight_id, others)
    return result.reshape(blocks * TOK_DEV, TOP).astype(jnp.int32)


def block_scale(stream_key, extent, cuts, smallest, top_value):
    gain, own = 1.0, jax.random.fold_in(stream_key, 6)
    for axis_at, shards_of in cuts:
        draws = jnp.exp(jax.random.uniform(jax.random.fold_in(own, axis_at), (shards_of,), jnp.float32, smallest / len(cuts), top_value / len(cuts)))
        gain = gain * jnp.repeat(draws, extent[axis_at] // shards_of).reshape([-1 if axis == axis_at else 1 for axis in range(len(extent))])
    return gain


def bell_draw(stream_key, shape, width, bound, cuts=(), kind=jnp.bfloat16):
    array = jax.random.normal(stream_key, shape, jnp.float32) * width
    if len(cuts) > 0:
        array = block_scale(stream_key, shape, cuts, -0.22, 0.18) * array
    return jnp.clip(array, min=-bound, max=bound).astype(kind)


def setup_inputs(seed: int = 0) -> dict:
    key_list = jax.random.split(jax.random.key(seed), 6)
    grad_out = bell_draw(key_list[0], (TOKENS, D), 1.0, 6.0, ((0, 256),))
    expert_ids = draw_expert_ids(jax.random.fold_in(key_list[5], 71), 0)
    route_weights = jnp.clip(0.049804688 + 0.4501953 * jax.random.uniform(key_list[2], (TOKENS, TOP), jnp.float32) ** block_scale(key_list[2], (TOKENS, TOP), ((0, 256),), -0.2, 0.2), 0.049804688, 0.5).astype(jnp.bfloat16)
    saved_preact = bell_draw(key_list[3], (FLIGHT, N_DP, N_EXPERT, CAP, 2 * FF), 1.0, 6.0, ((0, 8), (1, 32)))
    down_weight = bell_draw(key_list[4], (FLIGHT, FF, D), FF ** -0.5, 0.15625, ((0, 8), (1, 32)))
    return dict(grad_out=grad_out, expert_ids=expert_ids, route_weights=route_weights, saved_preact=saved_preact, down_weight=down_weight)


def slot_tables(block_ids, block_weights):
    labels = jnp.arange(FLIGHT, dtype=jnp.int32)
    hits = block_ids[:, :, None] == labels[None, None, :]
    member = jnp.any(hits, axis=1).astype(jnp.int32)
    chosen = jnp.sum(jnp.where(hits, block_weights.astype(jnp.float32)[:, :, None], jnp.float32(0.0)), axis=1)
    rank = jnp.cumsum(member, axis=0) - member
    where_to = jnp.where(member == 1, labels[None, :] * CAP + rank, FLIGHT * CAP).reshape(-1)
    token_of = jnp.broadcast_to(jnp.arange(block_ids.shape[0], dtype=jnp.int32)[:, None], member.shape).reshape(-1)
    slot_token = jnp.zeros((FLIGHT * CAP + 1,), jnp.int32).at[where_to].set(token_of)[:FLIGHT * CAP]
    slot_weight = jnp.zeros((FLIGHT * CAP + 1,), jnp.float32).at[where_to].set(chosen.reshape(-1))[:FLIGHT * CAP]
    return slot_token, slot_weight.astype(jnp.bfloat16), rank


def expert_side(gathered_rows, slot_weight, preact, weight):
    gate = preact[:, :FF].astype(jnp.float32)
    upper = preact[:, FF:].astype(jnp.float32)
    sig = jax.nn.sigmoid(gate)
    hidden = (gate * sig * upper).astype(jnp.bfloat16)
    act_grad = lax.dot_general(gathered_rows, weight, (((1,), (1,)), ((), ())), preferred_element_type=jnp.float32)
    slot_route = jnp.sum(act_grad * hidden.astype(jnp.float32), axis=1)
    scale = slot_weight.astype(jnp.float32)[:, None]
    dh_val = scale * act_grad
    gate_grad = dh_val * upper * sig * (1.0 + gate * (1.0 - sig))
    upper_grad = dh_val * gate * sig
    preact_grad = jnp.concatenate([gate_grad, upper_grad], axis=1).astype(jnp.bfloat16)
    scaled = (scale * hidden.astype(jnp.float32)).astype(jnp.bfloat16)
    partial_sum = jnp.dot(scaled.T, gathered_rows, preferred_element_type=jnp.float32)
    return preact_grad, slot_route, partial_sum


def reference(grad_out, expert_ids, route_weights, saved_preact, down_weight):
    grads = grad_out.reshape(N_DP, N_EXPERT, TOK_DEV, D)
    ids_all = expert_ids.reshape(N_DP, N_EXPERT, TOK_DEV, TOP)
    wts_all = route_weights.reshape(N_DP, N_EXPERT, TOK_DEV, TOP)
    saved = jnp.transpose(saved_preact, (1, 0, 2, 3, 4))

    def one_group(total, inputs):
        grads_g, ids_g, wts_g, saved_g = inputs
        slot_token, slot_weight, rank = jax.vmap(slot_tables)(ids_g, wts_g)
        picked = jax.vmap(lambda rows_s, toks: rows_s[toks])(grads_g, slot_token)
        valid = (slot_weight > 0)[:, :, None]
        picked = jnp.where(valid, picked, jnp.zeros_like(picked)).reshape(N_EXPERT, FLIGHT, CAP, D)
        weights_sw = slot_weight.reshape(N_EXPERT, FLIGHT, CAP)

        def one_expert(index):
            rows_e = picked[:, index].reshape(N_EXPERT * CAP, D)
            w_e = weights_sw[:, index].reshape(N_EXPERT * CAP)
            pre_e = saved_g[index].reshape(N_EXPERT * CAP, 2 * FF)
            return expert_side(rows_e, w_e, pre_e, down_weight[index])

        pre_grad, slot_route, partial_sum = lax.map(one_expert, jnp.arange(FLIGHT, dtype=jnp.int32))
        rounded = lax.optimization_barrier(partial_sum.astype(jnp.bfloat16))
        total = total + rounded.astype(jnp.float32)
        back = jnp.transpose(slot_route.reshape(FLIGHT, N_EXPERT, CAP), (1, 0, 2)).reshape(N_EXPERT, FLIGHT * CAP)

        def token_side(back_s, ids_s, rank_s):
            clipped = jnp.clip(ids_s, 0, FLIGHT - 1)
            rank_k = jnp.take_along_axis(rank_s, clipped, axis=1)
            index = jnp.where(ids_s < FLIGHT, ids_s * CAP + rank_k, FLIGHT * CAP)
            padded = jnp.concatenate([back_s, jnp.zeros((1,), jnp.float32)])
            return padded[index]

        route_g = jax.vmap(token_side)(back, ids_g, rank)
        return total, (pre_grad.reshape(FLIGHT, N_EXPERT, CAP, 2 * FF), route_g)

    start = jnp.zeros((FLIGHT, FF, D), jnp.float32)
    down_grad, outs = lax.scan(one_group, start, (grads, ids_all, wts_all, saved))
    pre_all, route_all = outs
    preact_grad = jnp.transpose(pre_all, (1, 0, 2, 3, 4))
    route_grad = route_all.reshape(TOKENS, TOP)
    return route_grad, preact_grad, down_grad
```

```python
import functools

import jax
import jax.numpy as jnp
from jax import lax
from jax.experimental import pallas as pl
from jax.experimental.pallas import tpu as pltpu
from jax.sharding import PartitionSpec as P

F32 = jnp.float32
BF16 = jnp.bfloat16
LANES = 128
TILE = 512
NY = 4
NZ = 8
VMEM_LIMIT = 40 * 1024 * 1024


def params(grid_rank):
    return pltpu.CompilerParams(
        dimension_semantics=("arbitrary",) * grid_rank, vmem_limit_bytes=VMEM_LIMIT
    )


def cost(flops, moved):
    return pl.CostEstimate(flops=flops, bytes_accessed=moved, transcendentals=0)


def whole(shape):
    return pl.BlockSpec(shape, lambda *_: (0,) * len(shape))


def table_kernel(flight, capacity, width, ids_ref, w_ref, g_ref, rows_ref, onehot_ref, rank_ref):
    ids = ids_ref[...]
    weights = w_ref[...].astype(F32)
    tokens = ids.shape[1]
    member, chosen = [], []
    for e in range(flight):
        hit = ids == e
        member.append(jnp.max(jnp.where(hit, 1.0, 0.0), axis=0, keepdims=True))
        chosen.append(jnp.sum(jnp.where(hit, weights, 0.0), axis=0, keepdims=True))
    member = jnp.concatenate(member, axis=0)
    before = lax.broadcasted_iota(jnp.int32, (tokens, tokens), 0) < lax.broadcasted_iota(
        jnp.int32, (tokens, tokens), 1
    )
    rank = jnp.dot(
        member.astype(BF16), jnp.where(before, 1.0, 0.0).astype(BF16), preferred_element_type=F32
    )
    rank = jnp.where(member > 0.0, rank, -1.0)
    rank_ref[...] = rank
    slot = lax.broadcasted_iota(jnp.int32, (capacity, tokens), 0).astype(F32)
    for e in range(flight):
        here = rank[e : e + 1, :] == slot
        onehot_ref[e * capacity : (e + 1) * capacity, :] = jnp.where(here, 1.0, 0.0).astype(BF16)
        column = jnp.sum(jnp.where(here, chosen[e], 0.0), axis=1, keepdims=True)
        rows_ref[e * capacity : (e + 1) * capacity, width:] = jnp.broadcast_to(
            column, (capacity, LANES)
        ).astype(BF16)
    onehot = onehot_ref[...]
    for at in range(0, width, TILE):
        rows_ref[:, at : at + TILE] = jnp.dot(
            onehot, g_ref[:, at : at + TILE], preferred_element_type=F32
        ).astype(BF16)


def tables(ids_t, weights_t, grad_out, flight, capacity, width):
    tokens = grad_out.shape[0]
    slots = flight * capacity
    return pl.pallas_call(
        functools.partial(table_kernel, flight, capacity, width),
        grid=(1,),
        in_specs=[
            whole(ids_t.shape),
            whole(weights_t.shape),
            pl.BlockSpec((tokens, width), lambda i: (0, 0)),
        ],
        out_specs=[whole((slots, width + LANES)), whole((slots, tokens)), whole((flight, tokens))],
        out_shape=[
            jax.ShapeDtypeStruct((slots, width + LANES), BF16),
            jax.ShapeDtypeStruct((slots, tokens), BF16),
            jax.ShapeDtypeStruct((flight, tokens), F32),
        ],
        compiler_params=params(1),
        cost_estimate=cost(2 * slots * tokens * width, 4 * tokens * width + 2 * slots * tokens),
        name="tables",
    )(ids_t, weights_t, grad_out)


def pick_kernel(onehot_ref, g_ref, rows_ref):
    rows_ref[...] = jnp.dot(onehot_ref[...], g_ref[...], preferred_element_type=F32).astype(BF16)


def pick(onehot, grad_out, start, width):
    slots, tokens = onehot.shape
    first = start // TILE
    return pl.pallas_call(
        pick_kernel,
        grid=(width // TILE,),
        in_specs=[
            whole(onehot.shape),
            pl.BlockSpec((tokens, TILE), lambda i: (0, first + i)),
        ],
        out_specs=pl.BlockSpec((slots, TILE), lambda i: (0, i)),
        out_shape=jax.ShapeDtypeStruct((slots, width), BF16),
        compiler_params=params(1),
        cost_estimate=cost(2 * slots * tokens * width, 4 * tokens * width + 2 * slots * tokens),
        name="pick",
    )(onehot, grad_out)


def hidden_kernel(gate_ref, up_ref, out_ref):
    gate = gate_ref[...].astype(F32)
    out_ref[...] = (gate * jax.nn.sigmoid(gate) * up_ref[...].astype(F32)).T.astype(BF16)


def hidden_transposed(preact):
    rows, both = preact.shape
    units = both // 2
    block = 256
    count = units // block
    return pl.pallas_call(
        hidden_kernel,
        grid=(count,),
        in_specs=[
            pl.BlockSpec((rows, block), lambda i: (0, i)),
            pl.BlockSpec((rows, block), lambda i: (0, count + i)),
        ],
        out_specs=pl.BlockSpec((block, rows), lambda i: (i, 0)),
        out_shape=jax.ShapeDtypeStruct((units, rows), BF16),
        compiler_params=params(1),
        cost_estimate=cost(10 * rows * units, 6 * rows * units),
        name="hidden",
    )(preact, preact)


def scale_kernel(w_ref, out_ref):
    out_ref[...] = w_ref[...].astype(F32).T[:8, :]


def scale_row(got, width):
    rows = got.shape[0]
    return pl.pallas_call(
        scale_kernel,
        grid=(1,),
        in_specs=[pl.BlockSpec((rows, LANES), lambda i: (0, width // LANES))],
        out_specs=whole((8, rows)),
        out_shape=jax.ShapeDtypeStruct((8, rows), F32),
        compiler_params=params(1),
        cost_estimate=cost(0, 2 * rows * LANES),
        name="scale",
    )(got)


def product(hidden_ref, scale_ref, rows_ref):
    hidden = hidden_ref[...]
    hidden = hidden.reshape(-1, hidden.shape[-1]).astype(F32)
    scaled = (hidden * scale_ref[0:1, :]).astype(BF16)
    return jnp.dot(scaled, rows_ref[...], preferred_element_type=F32)


def first_kernel(at_ref, hid_ref, scale_ref, rows_ref, down_ref, up_ref):
    value = product(hid_ref, scale_ref, rows_ref).astype(BF16)
    half = value.shape[0] // 2
    down_ref[...] = value[:half]
    up_ref[...] = value[half:]


def middle_kernel(at_ref, hid_d, hid_u, scale_ref, rows_ref, got_d, got_u, down_ref, up_ref):
    down = product(hid_d, scale_ref, rows_ref)
    up = product(hid_u, scale_ref, rows_ref)
    size, part = down.shape[0], got_d.shape[0]
    if part == size:
        down_ref[...] = (down + got_d[...].astype(F32)).astype(BF16)
        up_ref[...] = (up + got_u[...].astype(F32)).astype(BF16)
    else:
        down_ref[:part] = (down[:part] + got_d[...].astype(F32)).astype(BF16)
        down_ref[part:] = down[part:].astype(BF16)
        up_ref[:part] = up[:part].astype(BF16)
        up_ref[part:] = (up[part:] + got_u[...].astype(F32)).astype(BF16)


def last_kernel(at_ref, hid_ref, scale_ref, rows_ref, got_d, got_u, out_ref):
    own = product(hid_ref, scale_ref, rows_ref)
    out_ref[...] = (own + got_d[...].astype(F32) + got_u[...].astype(F32)).astype(BF16)


def neighbours(axis, step):
    pairs = []
    for z in range(NZ):
        for y in range(NY):
            to = ((z + step) % NZ, y) if axis == "z" else (z, (y + step) % NY)
            pairs.append((z * NY + y, to[0] * NY + to[1]))
    return pairs


def ring(axis, place, hidden, scale, rows, width):
    units, depth = hidden.shape
    shard = units // (NZ * NY)
    if axis == "z":
        size, slot = NZ, 0
        hidden = hidden.reshape(NZ, NY * shard, depth)
        hid_shape = (1, NY * shard, depth)
    else:
        size, slot = NY, 1
        hidden = hidden.reshape(NZ, NY, shard, depth)
        hid_shape = (NZ, 1, shard, depth)
    block = units // size
    half = size // 2
    tiles = width // TILE

    def hid(offset):
        def target(at):
            return (at[slot] + (offset + size)) & (size - 1)

        if axis == "z":
            return pl.BlockSpec(hid_shape, lambda i, at: (target(at), 0, 0))
        return pl.BlockSpec(hid_shape, lambda i, at: (0, target(at), 0, 0))

    def tile(n):
        return pl.BlockSpec((n, TILE), lambda i, at: (0, i))

    common = [pl.BlockSpec(scale.shape, lambda i, at: (0, 0)), tile(depth)]

    def call(kernel, offsets, arrived, outs, name):
        return pl.pallas_call(
            kernel,
            grid_spec=pltpu.PrefetchScalarGridSpec(
                num_scalar_prefetch=1,
                grid=(tiles,),
                in_specs=[hid(o) for o in offsets]
                + common
                + [tile(a.shape[0]) for a in arrived],
                out_specs=[tile(n) for n in outs],
            ),
            out_shape=[jax.ShapeDtypeStruct((n, width), BF16) for n in outs],
            compiler_params=params(1),
            cost_estimate=cost(
                2 * block * depth * width * len(offsets),
                2 * width * (depth + sum(outs) + sum(a.shape[0] for a in arrived)),
            ),
            name=name,
        )(place, *[hidden] * len(offsets), scale, rows, *arrived)

    def send(down, up):
        return [
            lax.ppermute(down, "dp", neighbours(axis, -1)),
            lax.ppermute(up, "dp", neighbours(axis, 1)),
        ]

    arrived = send(*call(first_kernel, [half], [], [block // 2] * 2, "first_" + axis))
    for s in range(1, half):
        arrived = send(
            *call(middle_kernel, [s - half, half - s], arrived, [block] * 2, "middle_" + axis)
        )
    return call(last_kernel, [0], arrived, [block], "last_" + axis)[0]


def exchange(part, axis):
    if axis == "z":
        size, groups = NZ, [[z * NY + y for z in range(NZ)] for y in range(NY)]
    else:
        size, groups = NY, [[z * NY + y for y in range(NY)] for z in range(NZ)]
    part = part.reshape(size, part.shape[0] // size, part.shape[1])
    return lax.all_to_all(
        part, "dp", split_axis=0, concat_axis=0, tiled=True, axis_index_groups=groups
    )


def sum_kernel(count_a, a_ref, b_ref, out_ref):
    step = pl.program_id(0)

    @pl.when(step < count_a)
    def _():
        out_ref[...] = jnp.sum(a_ref[...].astype(F32), axis=0)

    @pl.when(step >= count_a)
    def _():
        out_ref[...] = jnp.sum(b_ref[...].astype(F32), axis=0)


def sum_parts(a, b):
    shard = a.shape[1]
    count_a, count_b = a.shape[2] // TILE, b.shape[2] // TILE
    return pl.pallas_call(
        functools.partial(sum_kernel, count_a),
        grid=(count_a + count_b,),
        in_specs=[
            pl.BlockSpec((a.shape[0], shard, TILE), lambda i: (0, 0, jnp.minimum(i, count_a - 1))),
            pl.BlockSpec((b.shape[0], shard, TILE), lambda i: (0, 0, jnp.maximum(i - count_a, 0))),
        ],
        out_specs=pl.BlockSpec((shard, TILE), lambda i: (0, i)),
        out_shape=jax.ShapeDtypeStruct((shard, a.shape[2] + b.shape[2]), F32),
        compiler_params=params(1),
        cost_estimate=cost(a.size + b.size, 2 * (a.size + b.size) + 4 * shard * TILE * 8),
        name="sum_parts",
    )(a, b)


def act_kernel(
    width, units, block, rows_a, rows_b, weight_ref, gate_ref, up_ref, scale_ref, pre_ref, route_ref, total
):
    step = pl.program_id(0)
    last = (((1,), (1,)), ((), ()))
    act = lax.dot_general(
        rows_a[:, :width], weight_ref[:, :width], last, preferred_element_type=F32
    ) + lax.dot_general(rows_b[...], weight_ref[:, width:], last, preferred_element_type=F32)
    gate = gate_ref[...].astype(F32)
    up = up_ref[...].astype(F32)
    sig = jax.nn.sigmoid(gate)
    hidden = (gate * sig * up).astype(BF16).astype(F32)
    part = jnp.sum(act * hidden, axis=1, keepdims=True)

    @pl.when(step == 0)
    def _():
        total[...] = jnp.zeros_like(total)

    total[...] += jnp.broadcast_to(part, total.shape)
    dh = rows_a[:, width : width + 1].astype(F32) * act
    at = pl.multiple_of(step * block, block)
    pre_ref[:, pl.ds(at, block)] = (dh * up * sig * (1.0 + gate * (1.0 - sig))).astype(BF16)
    pre_ref[:, pl.ds(units + at, block)] = (dh * gate * sig).astype(BF16)

    @pl.when(step == pl.num_programs(0) - 1)
    def _():
        route_ref[...] = total[...].T[:8, :]


def act_side(rows_a, rows_b, weight, preact, scale, width):
    rows, both = preact.shape
    units = both // 2
    model = weight.shape[1]
    block = 256
    count = units // block
    return pl.pallas_call(
        functools.partial(act_kernel, width, units, block),
        grid=(count,),
        in_specs=[
            whole(rows_a.shape),
            whole(rows_b.shape),
            pl.BlockSpec((block, model), lambda i: (i, 0)),
            pl.BlockSpec((rows, block), lambda i: (0, i)),
            pl.BlockSpec((rows, block), lambda i: (0, count + i)),
            whole(scale.shape),
        ],
        out_specs=[whole((rows, both)), whole((8, rows))],
        out_shape=[
            jax.ShapeDtypeStruct((rows, both), BF16),
            jax.ShapeDtypeStruct((8, rows), F32),
        ],
        scratch_shapes=[pltpu.VMEM((rows, LANES), F32)],
        compiler_params=params(1),
        cost_estimate=cost(
            2 * rows * units * model, 2 * (units * model + rows * model + 2 * rows * both)
        ),
        name="act_side",
    )(rows_a, rows_b, weight, preact, preact, scale)


def combine_kernel(capacity, back_ref, ids_ref, rank_ref, out_ref):
    ids = ids_ref[...]
    back = back_ref[...]
    tokens = ids.shape[1]
    slot = lax.broadcasted_iota(jnp.int32, (capacity, tokens), 0).astype(F32)
    total = jnp.zeros(ids.shape, F32)
    for e in range(back.shape[0]):
        here = jnp.where(rank_ref[e : e + 1, :] == slot, 1.0, 0.0)
        value = jnp.dot(
            back, here, preferred_element_type=F32, precision=lax.Precision.HIGHEST
        )
        total = total + jnp.where(ids == e, value[e : e + 1, :], 0.0)
    out_ref[...] = total


def combine(back, ids_t, rank):
    return pl.pallas_call(
        functools.partial(combine_kernel, back.shape[1]),
        grid=(1,),
        in_specs=[whole(back.shape), whole(ids_t.shape), whole(rank.shape)],
        out_specs=whole(ids_t.shape),
        out_shape=jax.ShapeDtypeStruct(ids_t.shape, F32),
        compiler_params=params(1),
        cost_estimate=cost(2 * 64 * ids_t.size * 48, 12 * ids_t.size),
        name="combine",
    )(back, ids_t, rank)


def per_device(split, grad_out, expert_ids, route_weights, saved_preact, down_weight):
    flight = lax.axis_size("expert")
    capacity = saved_preact.shape[3]
    both = saved_preact.shape[4]
    slots = flight * capacity
    model = grad_out.shape[1]
    weight = lax.all_gather(down_weight[0], "dp", axis=0, tiled=True)
    ids_t = expert_ids.T
    at_dp = lax.axis_index("dp")
    place = jnp.stack([at_dp >> (NY.bit_length() - 1), at_dp & (NY - 1)]).astype(jnp.int32)
    rows_a, onehot, rank = tables(ids_t, route_weights.T, grad_out, flight, capacity, split)
    rows_b = pick(onehot, grad_out, split, model - split)

    def dispatch(rows):
        width = rows.shape[1]
        return lax.all_to_all(
            rows.reshape(flight, capacity, width), "expert", split_axis=0, concat_axis=0, tiled=True
        ).reshape(slots, width)

    preact = saved_preact.reshape(slots, both)
    hidden = hidden_transposed(preact)
    got_a = dispatch(rows_a)
    scale = scale_row(got_a, split)
    got_b = dispatch(rows_b)
    part_a = exchange(ring("z", place, hidden, scale, got_a, split), "y")
    part_b = exchange(ring("y", place, hidden, scale, got_b, model - split), "z")
    own = sum_parts(part_a, part_b)
    pre_grad, route = act_side(got_a, got_b, weight, preact, scale, split)
    back = lax.all_to_all(
        route[0].reshape(flight, capacity), "expert", split_axis=0, concat_axis=0, tiled=True
    )
    route_grad = combine(back, ids_t, rank).T
    return (route_grad, pre_grad.reshape(saved_preact.shape), own[None])


def solution(mesh):
    return jax.shard_map(
        functools.partial(per_device, 2560),
        mesh=mesh,
        in_specs=(
            P(("dp", "expert"), None),
            P(("dp", "expert"), None),
            P(("dp", "expert"), None),
            P("expert", "dp", None, None, None),
            P("expert", "dp", None),
        ),
        out_specs=(
            P(("dp", "expert"), None),
            P("expert", "dp", None, None, None),
            P("expert", "dp", None),
        ),
        check_vma=False,
    )
```

```python
import functools

import jax
import jax.numpy as jnp
from jax import lax
from jax.experimental import pallas as pl
from jax.experimental.pallas import tpu as pltpu
from jax.sharding import PartitionSpec as P

F32 = jnp.float32
BF16 = jnp.bfloat16
LANES = 128
TILE = 512
NY = 4
NZ = 8
ALONG_Z = [[z * NY + y for z in range(NZ)] for y in range(NY)]
ALONG_Y = [[z * NY + y for y in range(NY)] for z in range(NZ)]
MIB = 1024 * 1024


def params(grid_rank, mib=16):
    return pltpu.CompilerParams(
        dimension_semantics=("arbitrary",) * grid_rank, vmem_limit_bytes=mib * MIB
    )


def cost(flops, moved):
    return pl.CostEstimate(flops=flops, bytes_accessed=moved, transcendentals=0)


def whole(shape):
    return pl.BlockSpec(shape, lambda *_: (0,) * len(shape))


def table_kernel(flight, capacity, width, ids_ref, w_ref, g_ref, rows_ref, onehot_ref, rank_ref):
    ids = ids_ref[...]
    weights = w_ref[...].astype(F32)
    tokens = ids.shape[1]
    member, chosen = [], []
    for e in range(flight):
        hit = ids == e
        member.append(jnp.max(jnp.where(hit, 1.0, 0.0), axis=0, keepdims=True))
        chosen.append(jnp.sum(jnp.where(hit, weights, 0.0), axis=0, keepdims=True))
    member = jnp.concatenate(member, axis=0)
    before = lax.broadcasted_iota(jnp.int32, (tokens, tokens), 0) < lax.broadcasted_iota(
        jnp.int32, (tokens, tokens), 1
    )
    rank = jnp.dot(
        member.astype(BF16), jnp.where(before, 1.0, 0.0).astype(BF16), preferred_element_type=F32
    )
    rank = jnp.where(member > 0.0, rank, -1.0)
    rank_ref[...] = rank
    slot = lax.broadcasted_iota(jnp.int32, (capacity, tokens), 0).astype(F32)
    for e in range(flight):
        here = rank[e : e + 1, :] == slot
        onehot_ref[e * capacity : (e + 1) * capacity, :] = jnp.where(here, 1.0, 0.0).astype(BF16)
        column = jnp.sum(jnp.where(here, chosen[e], 0.0), axis=1, keepdims=True)
        rows_ref[e * capacity : (e + 1) * capacity, width:] = jnp.broadcast_to(
            column, (capacity, LANES)
        ).astype(BF16)
    onehot = onehot_ref[...]
    for at in range(0, width, TILE):
        rows_ref[:, at : at + TILE] = jnp.dot(
            onehot, g_ref[:, at : at + TILE], preferred_element_type=F32
        ).astype(BF16)


def tables(ids_t, weights_t, grad_out, flight, capacity, width):
    tokens = grad_out.shape[0]
    slots = flight * capacity
    return pl.pallas_call(
        functools.partial(table_kernel, flight, capacity, width),
        grid=(1,),
        in_specs=[
            whole(ids_t.shape),
            whole(weights_t.shape),
            pl.BlockSpec((tokens, width), lambda i: (0, 0)),
        ],
        out_specs=[whole((slots, width + LANES)), whole((slots, tokens)), whole((flight, tokens))],
        out_shape=[
            jax.ShapeDtypeStruct((slots, width + LANES), BF16),
            jax.ShapeDtypeStruct((slots, tokens), BF16),
            jax.ShapeDtypeStruct((flight, tokens), F32),
        ],
        compiler_params=params(1),
        cost_estimate=cost(2 * slots * tokens * width, 4 * tokens * width + 2 * slots * tokens),
        name="tables",
    )(ids_t, weights_t, grad_out)


def pick_kernel(onehot_ref, g_ref, rows_ref):
    rows_ref[...] = jnp.dot(onehot_ref[...], g_ref[...], preferred_element_type=F32).astype(BF16)


def pick(onehot, grad_out, start, width):
    slots, tokens = onehot.shape
    first = start // TILE
    return pl.pallas_call(
        pick_kernel,
        grid=(width // TILE,),
        in_specs=[
            whole(onehot.shape),
            pl.BlockSpec((tokens, TILE), lambda i: (0, first + i)),
        ],
        out_specs=pl.BlockSpec((slots, TILE), lambda i: (0, i)),
        out_shape=jax.ShapeDtypeStruct((slots, width), BF16),
        compiler_params=params(1),
        cost_estimate=cost(2 * slots * tokens * width, 4 * tokens * width + 2 * slots * tokens),
        name="pick",
    )(onehot, grad_out)


def same_kernel(array_ref, after_ref, out_ref):
    pass


def hold(array, after):
    return pl.pallas_call(
        same_kernel,
        in_specs=[pl.BlockSpec(memory_space=pl.ANY)] * 2,
        out_specs=pl.BlockSpec(memory_space=pl.ANY),
        out_shape=jax.ShapeDtypeStruct(array.shape, array.dtype),
        input_output_aliases={0: 0},
        name="hold",
    )(array, after)


def hidden_kernel(gate_ref, up_ref, after_ref, out_ref):
    gate = gate_ref[...].astype(F32)
    out_ref[...] = (gate * jax.nn.sigmoid(gate) * up_ref[...].astype(F32)).T.astype(BF16)


def hidden_transposed(preact, after):
    rows, both = preact.shape
    units = both // 2
    block = 256
    count = units // block
    return pl.pallas_call(
        hidden_kernel,
        grid=(count,),
        in_specs=[
            pl.BlockSpec((rows, block), lambda i: (0, i)),
            pl.BlockSpec((rows, block), lambda i: (0, count + i)),
            pl.BlockSpec(memory_space=pl.ANY),
        ],
        out_specs=pl.BlockSpec((block, rows), lambda i: (i, 0)),
        out_shape=jax.ShapeDtypeStruct((units, rows), BF16),
        compiler_params=params(1),
        cost_estimate=cost(10 * rows * units, 6 * rows * units),
        name="hidden",
    )(preact, preact, after)


def scale_kernel(w_ref, out_ref):
    out_ref[...] = w_ref[...].astype(F32).T[:8, :]


def scale_row(got, width):
    rows = got.shape[0]
    return pl.pallas_call(
        scale_kernel,
        grid=(1,),
        in_specs=[pl.BlockSpec((rows, LANES), lambda i: (0, width // LANES))],
        out_specs=whole((8, rows)),
        out_shape=jax.ShapeDtypeStruct((8, rows), F32),
        compiler_params=params(1),
        cost_estimate=cost(0, 2 * rows * LANES),
        name="scale",
    )(got)


def product(hidden_ref, scale_ref, rows_ref):
    hidden = hidden_ref[...]
    hidden = hidden.reshape(-1, hidden.shape[-1]).astype(F32)
    scaled = (hidden * scale_ref[0:1, :]).astype(BF16)
    return jnp.dot(scaled, rows_ref[...], preferred_element_type=F32)


def first_kernel(at_ref, hid_ref, scale_ref, rows_ref, after_ref, down_ref, up_ref):
    value = product(hid_ref, scale_ref, rows_ref).astype(BF16)
    half = value.shape[0] // 2
    down_ref[...] = value[:half]
    up_ref[...] = value[half:]


def middle_kernel(at_ref, hid_d, hid_u, scale_ref, rows_ref, got_d, got_u, after_ref, down_ref, up_ref):
    down = product(hid_d, scale_ref, rows_ref)
    up = product(hid_u, scale_ref, rows_ref)
    size, part = down.shape[0], got_d.shape[0]
    if part == size:
        down_ref[...] = (down + got_d[...].astype(F32)).astype(BF16)
        up_ref[...] = (up + got_u[...].astype(F32)).astype(BF16)
    else:
        down_ref[:part] = (down[:part] + got_d[...].astype(F32)).astype(BF16)
        down_ref[part:] = down[part:].astype(BF16)
        up_ref[:part] = up[:part].astype(BF16)
        up_ref[part:] = (up[part:] + got_u[...].astype(F32)).astype(BF16)


def last_kernel(at_ref, hid_ref, scale_ref, rows_ref, got_d, got_u, after_ref, out_ref):
    own = product(hid_ref, scale_ref, rows_ref)
    out_ref[...] = (own + got_d[...].astype(F32) + got_u[...].astype(F32)).astype(BF16)


def neighbours(axis, step):
    pairs = []
    for z in range(NZ):
        for y in range(NY):
            to = ((z + step) % NZ, y) if axis == "z" else (z, (y + step) % NY)
            pairs.append((z * NY + y, to[0] * NY + to[1]))
    return pairs


def ring(axis, place, hidden, scale, rows, width):
    units, depth = hidden.shape
    shard = units // (NZ * NY)
    if axis == "z":
        size, slot = NZ, 0
        hidden = hidden.reshape(NZ, NY * shard, depth)
        hid_shape = (1, NY * shard, depth)
    else:
        size, slot = NY, 1
        hidden = hidden.reshape(NZ, NY, shard, depth)
        hid_shape = (NZ, 1, shard, depth)
    block = units // size
    half = size // 2

    def hid(offset):
        def target(at):
            return (at[slot] + (offset + size)) & (size - 1)

        if axis == "z":
            return pl.BlockSpec(hid_shape, lambda i, at: (target(at), 0, 0))
        return pl.BlockSpec(hid_shape, lambda i, at: (0, target(at), 0, 0))

    tiles = 2

    def tile(n):
        return pl.BlockSpec((n, width // tiles), lambda i, at: (0, i))

    common = [pl.BlockSpec(scale.shape, lambda i, at: (0, 0)), tile(depth)]

    def call(kernel, offsets, arrived, outs, name, after):
        return pl.pallas_call(
            kernel,
            grid_spec=pltpu.PrefetchScalarGridSpec(
                num_scalar_prefetch=1,
                grid=(tiles,),
                in_specs=[hid(o) for o in offsets]
                + common
                + [tile(a.shape[0]) for a in arrived]
                + [pl.BlockSpec(memory_space=pl.ANY)],
                out_specs=[tile(n) for n in outs],
            ),
            out_shape=[jax.ShapeDtypeStruct((n, width), BF16) for n in outs],
            compiler_params=params(1),
            cost_estimate=cost(block * width, block),
            name=name,
        )(place, *[hidden] * len(offsets), scale, rows, *arrived, after)

    def step(number, arrived, after):
        if number == 0:
            made = call(first_kernel, [half], [], [block // 2] * 2, "first_" + axis, after)
        elif number < half:
            made = call(
                middle_kernel,
                [number - half, half - number],
                arrived,
                [block] * 2,
                "middle_" + axis,
                after,
            )
        else:
            return call(last_kernel, [0], arrived, [block], "last_" + axis, after)[0], None
        return made[0], [
            lax.ppermute(made[0], "dp", neighbours(axis, -1)),
            lax.ppermute(made[1], "dp", neighbours(axis, 1)),
        ]

    return step


def exchange(part, axis):
    size, groups = (NZ, ALONG_Z) if axis == "z" else (NY, ALONG_Y)
    part = part.reshape(size, part.shape[0] // size, part.shape[1])
    return lax.all_to_all(
        part, "dp", split_axis=0, concat_axis=0, tiled=True, axis_index_groups=groups
    )


def sum_kernel(firsts, *refs):
    out_ref = refs[-1]
    tile = pl.program_id(0)
    for k, part in enumerate(refs[:-1]):

        @pl.when((tile >= firsts[k]) & (tile < firsts[k + 1]))
        def _():
            out_ref[...] = jnp.sum(part[...].astype(F32), axis=0)


def sum_parts(parts):
    shard = parts[0].shape[1]
    counts = [part.shape[2] // TILE for part in parts]
    firsts = [sum(counts[:k]) for k in range(len(counts) + 1)]

    def spec(part, first, count):
        return pl.BlockSpec(
            (part.shape[0], shard, TILE), lambda i: (0, 0, jnp.clip(i - first, 0, count - 1))
        )

    return pl.pallas_call(
        functools.partial(sum_kernel, firsts),
        grid=(firsts[-1],),
        in_specs=[spec(*each) for each in zip(parts, firsts, counts)],
        out_specs=pl.BlockSpec((shard, TILE), lambda i: (0, i)),
        out_shape=jax.ShapeDtypeStruct((shard, firsts[-1] * TILE), F32),
        compiler_params=params(1),
        cost_estimate=cost(
            sum(part.size for part in parts),
            sum(2 * part.size for part in parts) + 4 * shard * firsts[-1] * TILE,
        ),
        name="sum_parts",
    )(*parts)


def act_kernel(starts, units, *refs):
    rows = refs[: len(starts) - 1]
    weight_ref, gate_ref, up_ref, _, pre_ref, route_ref, total, held = refs[len(starts) - 1 :]
    step = pl.program_id(0)
    ny, nz, shard, _ = weight_ref.shape
    block = ny * nz * shard
    for z in range(nz):
        for y in range(ny):
            at = (z * ny + y) * shard
            held[at : at + shard, :] = weight_ref[y, z]
    act = None
    for part, start, end in zip(rows, starts, starts[1:]):
        more = lax.dot_general(
            part[:, : end - start],
            held[:, start:end],
            (((1,), (1,)), ((), ())),
            preferred_element_type=F32,
        )
        act = more if act is None else act + more
    gate = gate_ref[...].astype(F32)
    up = up_ref[...].astype(F32)
    sig = jax.nn.sigmoid(gate)
    hidden = (gate * sig * up).astype(BF16).astype(F32)
    part = jnp.sum(act * hidden, axis=1, keepdims=True)

    @pl.when(step == 0)
    def _():
        total[...] = jnp.zeros_like(total)

    total[...] += jnp.broadcast_to(part, total.shape)
    dh = rows[0][:, starts[1] : starts[1] + 1].astype(F32) * act
    at = pl.multiple_of(step * block, block)
    pre_ref[:, pl.ds(at, block)] = (dh * up * sig * (1.0 + gate * (1.0 - sig))).astype(BF16)
    pre_ref[:, pl.ds(units + at, block)] = (dh * gate * sig).astype(BF16)

    @pl.when(step == pl.num_programs(0) - 1)
    def _():
        route_ref[...] = total[...].T[:8, :]


def act_side(got, starts, weight, preact, after):
    rows, both = preact.shape
    units = both // 2
    ny, nz, shard, model = weight.shape
    each = 2
    block = ny * each * shard
    count = units // block
    return pl.pallas_call(
        functools.partial(act_kernel, starts, units),
        grid=(count,),
        in_specs=[
            *[whole(part.shape) for part in got],
            pl.BlockSpec((ny, each, shard, model), lambda i: (0, i, 0, 0)),
            pl.BlockSpec((rows, block), lambda i: (0, i)),
            pl.BlockSpec((rows, block), lambda i: (0, count + i)),
            pl.BlockSpec(memory_space=pl.ANY),
        ],
        out_specs=[whole((rows, both)), whole((8, rows))],
        out_shape=[
            jax.ShapeDtypeStruct((rows, both), BF16),
            jax.ShapeDtypeStruct((8, rows), F32),
        ],
        scratch_shapes=[pltpu.VMEM((rows, LANES), F32), pltpu.VMEM((block, model), BF16)],
        compiler_params=params(1, 44),
        cost_estimate=cost(
            2 * rows * units * model, 2 * (units * model + rows * model + 2 * rows * both)
        ),
        name="act_side",
    )(*got, weight, preact, preact, after)


def combine_kernel(capacity, back_ref, ids_ref, rank_ref, out_ref):
    ids = ids_ref[...]
    back = back_ref[...]
    tokens = ids.shape[1]
    slot = lax.broadcasted_iota(jnp.int32, (capacity, tokens), 0).astype(F32)
    total = jnp.zeros(ids.shape, F32)
    for e in range(back.shape[0]):
        here = jnp.where(rank_ref[e : e + 1, :] == slot, 1.0, 0.0)
        value = jnp.dot(
            back, here, preferred_element_type=F32, precision=lax.Precision.HIGHEST
        )
        total = total + jnp.where(ids == e, value[e : e + 1, :], 0.0)
    out_ref[...] = total


def combine(back, ids_t, rank):
    return pl.pallas_call(
        functools.partial(combine_kernel, back.shape[1]),
        grid=(1,),
        in_specs=[whole(back.shape), whole(ids_t.shape), whole(rank.shape)],
        out_specs=whole(ids_t.shape),
        out_shape=jax.ShapeDtypeStruct(ids_t.shape, F32),
        compiler_params=params(1),
        cost_estimate=cost(2 * 64 * ids_t.size * 48, 12 * ids_t.size),
        name="combine",
    )(back, ids_t, rank)


def per_device(chunks, order, grad_out, expert_ids, route_weights, saved_preact, down_weight):
    flight = lax.axis_size("expert")
    capacity = saved_preact.shape[3]
    both = saved_preact.shape[4]
    slots = flight * capacity
    starts = [sum(width for _, width in chunks[:k]) for k in range(len(chunks) + 1)]
    weight = lax.all_gather(down_weight[0], "dp", axis=0, axis_index_groups=ALONG_Z)
    ids_t = expert_ids.T
    at_dp = lax.axis_index("dp")
    place = jnp.stack([at_dp >> (NY.bit_length() - 1), at_dp & (NY - 1)]).astype(jnp.int32)
    first, onehot, rank = tables(
        ids_t, route_weights.T, grad_out, flight, capacity, chunks[0][1]
    )
    rows = [first] + [
        pick(onehot, grad_out, start, width) for start, (_, width) in zip(starts[1:], chunks[1:])
    ]
    preact = saved_preact.reshape(slots, both)
    hidden = hidden_transposed(preact, rows[-1])

    def dispatch(part):
        width = part.shape[1]
        return lax.all_to_all(
            part.reshape(flight, capacity, width), "expert", split_axis=0, concat_axis=0, tiled=True
        ).reshape(slots, width)

    got = [dispatch(first)]
    scale = scale_row(got[0], starts[1])
    made = scale
    steps, arrived, number, parts = {}, {}, [0] * len(chunks), {}
    for item in order:
        if item == "gather":
            weight = lax.all_gather(hold(weight, made), "dp", axis=0, axis_index_groups=ALONG_Y)
            continue
        if item == "act":
            pre_grad, route = act_side(got, starts, weight, preact, made)
            made = route
            continue
        axis, width = chunks[item]
        if number[item] == 0:
            steps[item] = ring(axis, place, hidden, scale, got[item], width)
            arrived[item] = []
        made, arrived[item] = steps[item](number[item], arrived[item], made)
        if number[item] == 0 and item + 1 < len(chunks):
            got.append(dispatch(hold(rows[item + 1], made)))
        number[item] += 1
        if arrived[item] is None:
            parts[item] = exchange(made, "y" if axis == "z" else "z")
    own = sum_parts([parts[k] for k in range(len(chunks))])
    back = lax.all_to_all(
        route[0].reshape(flight, capacity), "expert", split_axis=0, concat_axis=0, tiled=True
    )
    route_grad = combine(back, ids_t, rank).T
    return (route_grad, pre_grad.reshape(saved_preact.shape), own[None])


CHUNKS = (("z", 2048), ("z", 2048))
ORDER = (0, "gather", 0, 1, 0, 1, 0, 1, 0, 1, "act", 1)


def solution(mesh):
    return jax.shard_map(
        functools.partial(per_device, CHUNKS, ORDER),
        mesh=mesh,
        in_specs=(
            P(("dp", "expert"), None),
            P(("dp", "expert"), None),
            P(("dp", "expert"), None),
            P("expert", "dp", None, None, None),
            P("expert", "dp", None),
        ),
        out_specs=(
            P(("dp", "expert"), None),
            P("expert", "dp", None, None, None),
            P("expert", "dp", None),
        ),
        check_vma=False,
    )
```

```python
import functools

import jax
import jax.numpy as jnp
from jax import lax
from jax.experimental import pallas as pl
from jax.experimental.pallas import tpu as pltpu
from jax.sharding import PartitionSpec as P

F32 = jnp.float32
BF16 = jnp.bfloat16
LANES = 128
TILE = 512
NY = 4
NZ = 8
ALONG_Z = [[z * NY + y for z in range(NZ)] for y in range(NY)]
ALONG_Y = [[z * NY + y for y in range(NY)] for z in range(NZ)]
MIB = 1024 * 1024


def params(grid_rank, mib=16):
    return pltpu.CompilerParams(
        dimension_semantics=("arbitrary",) * grid_rank, vmem_limit_bytes=mib * MIB
    )


def cost(flops, moved):
    return pl.CostEstimate(flops=flops, bytes_accessed=moved, transcendentals=0)


def whole(shape):
    return pl.BlockSpec(shape, lambda *_: (0,) * len(shape))


def table_kernel(flight, capacity, width, ids_ref, w_ref, g_ref, rows_ref, onehot_ref, rank_ref):
    ids = ids_ref[...]
    weights = w_ref[...].astype(F32)
    tokens = ids.shape[1]
    member, chosen = [], []
    for e in range(flight):
        hit = ids == e
        member.append(jnp.max(jnp.where(hit, 1.0, 0.0), axis=0, keepdims=True))
        chosen.append(jnp.sum(jnp.where(hit, weights, 0.0), axis=0, keepdims=True))
    member = jnp.concatenate(member, axis=0)
    before = lax.broadcasted_iota(jnp.int32, (tokens, tokens), 0) < lax.broadcasted_iota(
        jnp.int32, (tokens, tokens), 1
    )
    rank = jnp.dot(
        member.astype(BF16), jnp.where(before, 1.0, 0.0).astype(BF16), preferred_element_type=F32
    )
    rank = jnp.where(member > 0.0, rank, -1.0)
    rank_ref[...] = rank
    slot = lax.broadcasted_iota(jnp.int32, (capacity, tokens), 0).astype(F32)
    for e in range(flight):
        here = rank[e : e + 1, :] == slot
        onehot_ref[e * capacity : (e + 1) * capacity, :] = jnp.where(here, 1.0, 0.0).astype(BF16)
        column = jnp.sum(jnp.where(here, chosen[e], 0.0), axis=1, keepdims=True)
        rows_ref[e * capacity : (e + 1) * capacity, width:] = jnp.broadcast_to(
            column, (capacity, LANES)
        ).astype(BF16)
    onehot = onehot_ref[...]
    for at in range(0, width, TILE):
        rows_ref[:, at : at + TILE] = jnp.dot(
            onehot, g_ref[:, at : at + TILE], preferred_element_type=F32
        ).astype(BF16)


def tables(ids_t, weights_t, grad_out, flight, capacity, width):
    tokens = grad_out.shape[0]
    slots = flight * capacity
    return pl.pallas_call(
        functools.partial(table_kernel, flight, capacity, width),
        grid=(1,),
        in_specs=[
            whole(ids_t.shape),
            whole(weights_t.shape),
            pl.BlockSpec((tokens, width), lambda i: (0, 0)),
        ],
        out_specs=[whole((slots, width + LANES)), whole((slots, tokens)), whole((flight, tokens))],
        out_shape=[
            jax.ShapeDtypeStruct((slots, width + LANES), BF16),
            jax.ShapeDtypeStruct((slots, tokens), BF16),
            jax.ShapeDtypeStruct((flight, tokens), F32),
        ],
        compiler_params=params(1),
        cost_estimate=cost(2 * slots * tokens * width, 4 * tokens * width + 2 * slots * tokens),
        name="tables",
    )(ids_t, weights_t, grad_out)


def pick_kernel(onehot_ref, g_ref, rows_ref):
    rows_ref[...] = jnp.dot(onehot_ref[...], g_ref[...], preferred_element_type=F32).astype(BF16)


def pick(onehot, grad_out, start, width):
    slots, tokens = onehot.shape
    first = start // TILE
    return pl.pallas_call(
        pick_kernel,
        grid=(width // TILE,),
        in_specs=[
            whole(onehot.shape),
            pl.BlockSpec((tokens, TILE), lambda i: (0, first + i)),
        ],
        out_specs=pl.BlockSpec((slots, TILE), lambda i: (0, i)),
        out_shape=jax.ShapeDtypeStruct((slots, width), BF16),
        compiler_params=params(1),
        cost_estimate=cost(2 * slots * tokens * width, 4 * tokens * width + 2 * slots * tokens),
        name="pick",
    )(onehot, grad_out)


def same_kernel(array_ref, after_ref, out_ref):
    pass


def hold(array, after):
    return pl.pallas_call(
        same_kernel,
        in_specs=[pl.BlockSpec(memory_space=pl.ANY)] * 2,
        out_specs=pl.BlockSpec(memory_space=pl.ANY),
        out_shape=jax.ShapeDtypeStruct(array.shape, array.dtype),
        input_output_aliases={0: 0},
        name="hold",
    )(array, after)


def hidden_kernel(gate_ref, up_ref, after_ref, out_ref):
    gate = gate_ref[...].astype(F32)
    out_ref[...] = (gate * jax.nn.sigmoid(gate) * up_ref[...].astype(F32)).T.astype(BF16)


def hidden_transposed(preact, after):
    rows, both = preact.shape
    units = both // 2
    block = 256
    count = units // block
    return pl.pallas_call(
        hidden_kernel,
        grid=(count,),
        in_specs=[
            pl.BlockSpec((rows, block), lambda i: (0, i)),
            pl.BlockSpec((rows, block), lambda i: (0, count + i)),
            pl.BlockSpec(memory_space=pl.ANY),
        ],
        out_specs=pl.BlockSpec((block, rows), lambda i: (i, 0)),
        out_shape=jax.ShapeDtypeStruct((units, rows), BF16),
        compiler_params=params(1),
        cost_estimate=cost(10 * rows * units, 6 * rows * units),
        name="hidden",
    )(preact, preact, after)


def scale_kernel(w_ref, out_ref):
    out_ref[...] = w_ref[...].astype(F32).T[:8, :]


def scale_row(got, width):
    rows = got.shape[0]
    return pl.pallas_call(
        scale_kernel,
        grid=(1,),
        in_specs=[pl.BlockSpec((rows, LANES), lambda i: (0, width // LANES))],
        out_specs=whole((8, rows)),
        out_shape=jax.ShapeDtypeStruct((8, rows), F32),
        compiler_params=params(1),
        cost_estimate=cost(0, 2 * rows * LANES),
        name="scale",
    )(got)


def product(hidden_ref, scale_ref, rows_ref):
    hidden = hidden_ref[...]
    hidden = hidden.reshape(-1, hidden.shape[-1]).astype(F32)
    scaled = (hidden * scale_ref[0:1, :]).astype(BF16)
    return jnp.dot(scaled, rows_ref[...], preferred_element_type=F32)


def first_kernel(at_ref, hid_ref, scale_ref, rows_ref, after_ref, down_ref, up_ref):
    value = product(hid_ref, scale_ref, rows_ref).astype(BF16)
    half = value.shape[0] // 2
    down_ref[...] = value[:half]
    up_ref[...] = value[half:]


def middle_kernel(at_ref, hid_d, hid_u, scale_ref, rows_ref, got_d, got_u, after_ref, down_ref, up_ref):
    down = product(hid_d, scale_ref, rows_ref)
    up = product(hid_u, scale_ref, rows_ref)
    size, part = down.shape[0], got_d.shape[0]
    if part == size:
        down_ref[...] = (down + got_d[...].astype(F32)).astype(BF16)
        up_ref[...] = (up + got_u[...].astype(F32)).astype(BF16)
    else:
        down_ref[:part] = (down[:part] + got_d[...].astype(F32)).astype(BF16)
        down_ref[part:] = down[part:].astype(BF16)
        up_ref[:part] = up[:part].astype(BF16)
        up_ref[part:] = (up[part:] + got_u[...].astype(F32)).astype(BF16)


def last_kernel(at_ref, hid_ref, scale_ref, rows_ref, got_d, got_u, after_ref, out_ref):
    own = product(hid_ref, scale_ref, rows_ref)
    out_ref[...] = (own + got_d[...].astype(F32) + got_u[...].astype(F32)).astype(BF16)


def neighbours(axis, step):
    pairs = []
    for z in range(NZ):
        for y in range(NY):
            to = ((z + step) % NZ, y) if axis == "z" else (z, (y + step) % NY)
            pairs.append((z * NY + y, to[0] * NY + to[1]))
    return pairs


def ring(axis, place, hidden, scale, rows, width):
    units, depth = hidden.shape
    shard = units // (NZ * NY)
    if axis == "z":
        size, slot = NZ, 0
        hidden = hidden.reshape(NZ, NY * shard, depth)
        hid_shape = (1, NY * shard, depth)
    else:
        size, slot = NY, 1
        hidden = hidden.reshape(NZ, NY, shard, depth)
        hid_shape = (NZ, 1, shard, depth)
    block = units // size
    half = size // 2

    def hid(offset):
        def target(at):
            return (at[slot] + (offset + size)) & (size - 1)

        if axis == "z":
            return pl.BlockSpec(hid_shape, lambda i, at: (target(at), 0, 0))
        return pl.BlockSpec(hid_shape, lambda i, at: (0, target(at), 0, 0))

    tiles = 2

    def tile(n):
        return pl.BlockSpec((n, width // tiles), lambda i, at: (0, i))

    common = [pl.BlockSpec(scale.shape, lambda i, at: (0, 0)), tile(depth)]

    def call(kernel, offsets, arrived, outs, name, after):
        return pl.pallas_call(
            kernel,
            grid_spec=pltpu.PrefetchScalarGridSpec(
                num_scalar_prefetch=1,
                grid=(tiles,),
                in_specs=[hid(o) for o in offsets]
                + common
                + [tile(a.shape[0]) for a in arrived]
                + [pl.BlockSpec(memory_space=pl.ANY)],
                out_specs=[tile(n) for n in outs],
            ),
            out_shape=[jax.ShapeDtypeStruct((n, width), BF16) for n in outs],
            compiler_params=params(1),
            cost_estimate=cost(block * width, block),
            name=name,
        )(place, *[hidden] * len(offsets), scale, rows, *arrived, after)

    def step(number, arrived, after):
        if number == 0:
            made = call(first_kernel, [half], [], [block // 2] * 2, "first_" + axis, after)
        elif number < half:
            made = call(
                middle_kernel,
                [number - half, half - number],
                arrived,
                [block] * 2,
                "middle_" + axis,
                after,
            )
        else:
            return call(last_kernel, [0], arrived, [block], "last_" + axis, after)[0], None
        return made[0], [
            lax.ppermute(made[0], "dp", neighbours(axis, -1)),
            lax.ppermute(made[1], "dp", neighbours(axis, 1)),
        ]

    return step


def exchange(part, axis):
    size, groups = (NZ, ALONG_Z) if axis == "z" else (NY, ALONG_Y)
    part = part.reshape(size, part.shape[0] // size, part.shape[1])
    return lax.all_to_all(
        part, "dp", split_axis=0, concat_axis=0, tiled=True, axis_index_groups=groups
    )


def sum_kernel(firsts, *refs):
    out_ref = refs[-1]
    tile = pl.program_id(0)
    for k, part in enumerate(refs[:-1]):

        @pl.when((tile >= firsts[k]) & (tile < firsts[k + 1]))
        def _():
            out_ref[...] = jnp.sum(part[...].astype(F32), axis=0)


def sum_parts(parts):
    shard = parts[0].shape[1]
    counts = [part.shape[2] // TILE for part in parts]
    firsts = [sum(counts[:k]) for k in range(len(counts) + 1)]

    def spec(part, first, count):
        return pl.BlockSpec(
            (part.shape[0], shard, TILE), lambda i: (0, 0, jnp.clip(i - first, 0, count - 1))
        )

    return pl.pallas_call(
        functools.partial(sum_kernel, firsts),
        grid=(firsts[-1],),
        in_specs=[spec(*each) for each in zip(parts, firsts, counts)],
        out_specs=pl.BlockSpec((shard, TILE), lambda i: (0, i)),
        out_shape=jax.ShapeDtypeStruct((shard, firsts[-1] * TILE), F32),
        compiler_params=params(1),
        cost_estimate=cost(
            sum(part.size for part in parts),
            sum(2 * part.size for part in parts) + 4 * shard * firsts[-1] * TILE,
        ),
        name="sum_parts",
    )(*parts)


def act_kernel(starts, units, *refs):
    rows = refs[: len(starts) - 1]
    weight_ref, gate_ref, up_ref, _, pre_ref, route_ref, total, held = refs[len(starts) - 1 :]
    step = pl.program_id(0)
    ny, nz, shard, _ = weight_ref.shape
    block = ny * nz * shard
    for z in range(nz):
        for y in range(ny):
            at = (z * ny + y) * shard
            held[at : at + shard, :] = weight_ref[y, z]
    act = None
    for part, start, end in zip(rows, starts, starts[1:]):
        more = lax.dot_general(
            part[:, : end - start],
            held[:, start:end],
            (((1,), (1,)), ((), ())),
            preferred_element_type=F32,
        )
        act = more if act is None else act + more
    gate = gate_ref[...].astype(F32)
    up = up_ref[...].astype(F32)
    sig = jax.nn.sigmoid(gate)
    hidden = (gate * sig * up).astype(BF16).astype(F32)
    part = jnp.sum(act * hidden, axis=1, keepdims=True)

    @pl.when(step == 0)
    def _():
        total[...] = jnp.zeros_like(total)

    total[...] += jnp.broadcast_to(part, total.shape)
    dh = rows[0][:, starts[1] : starts[1] + 1].astype(F32) * act
    at = pl.multiple_of(step * block, block)
    pre_ref[:, pl.ds(at, block)] = (dh * up * sig * (1.0 + gate * (1.0 - sig))).astype(BF16)
    pre_ref[:, pl.ds(units + at, block)] = (dh * gate * sig).astype(BF16)

    @pl.when(step == pl.num_programs(0) - 1)
    def _():
        route_ref[...] = total[...].T[:8, :]


def act_side(got, starts, weight, preact, after):
    rows, both = preact.shape
    units = both // 2
    ny, nz, shard, model = weight.shape
    each = 2
    block = ny * each * shard
    count = units // block
    return pl.pallas_call(
        functools.partial(act_kernel, starts, units),
        grid=(count,),
        in_specs=[
            *[whole(part.shape) for part in got],
            pl.BlockSpec((ny, each, shard, model), lambda i: (0, i, 0, 0)),
            pl.BlockSpec((rows, block), lambda i: (0, i)),
            pl.BlockSpec((rows, block), lambda i: (0, count + i)),
            pl.BlockSpec(memory_space=pl.ANY),
        ],
        out_specs=[whole((rows, both)), whole((8, rows))],
        out_shape=[
            jax.ShapeDtypeStruct((rows, both), BF16),
            jax.ShapeDtypeStruct((8, rows), F32),
        ],
        scratch_shapes=[pltpu.VMEM((rows, LANES), F32), pltpu.VMEM((block, model), BF16)],
        compiler_params=params(1, 44),
        cost_estimate=cost(
            2 * rows * units * model, 2 * (units * model + rows * model + 2 * rows * both)
        ),
        name="act_side",
    )(*got, weight, preact, preact, after)


def combine_kernel(capacity, back_ref, ids_ref, rank_ref, out_ref):
    ids = ids_ref[...]
    back = back_ref[...]
    tokens = ids.shape[1]
    slot = lax.broadcasted_iota(jnp.int32, (capacity, tokens), 0).astype(F32)
    total = jnp.zeros(ids.shape, F32)
    for e in range(back.shape[0]):
        here = jnp.where(rank_ref[e : e + 1, :] == slot, 1.0, 0.0)
        value = jnp.dot(
            back, here, preferred_element_type=F32, precision=lax.Precision.HIGHEST
        )
        total = total + jnp.where(ids == e, value[e : e + 1, :], 0.0)
    out_ref[...] = total


def combine(back, ids_t, rank):
    return pl.pallas_call(
        functools.partial(combine_kernel, back.shape[1]),
        grid=(1,),
        in_specs=[whole(back.shape), whole(ids_t.shape), whole(rank.shape)],
        out_specs=whole(ids_t.shape),
        out_shape=jax.ShapeDtypeStruct(ids_t.shape, F32),
        compiler_params=params(1),
        cost_estimate=cost(2 * 64 * ids_t.size * 48, 12 * ids_t.size),
        name="combine",
    )(back, ids_t, rank)


def per_device(chunks, order, grad_out, expert_ids, route_weights, saved_preact, down_weight):
    flight = lax.axis_size("expert")
    capacity = saved_preact.shape[3]
    both = saved_preact.shape[4]
    slots = flight * capacity
    starts = [sum(width for _, width in chunks[:k]) for k in range(len(chunks) + 1)]
    weight = lax.all_gather(down_weight[0], "dp", axis=0, axis_index_groups=ALONG_Z)
    ids_t = expert_ids.T
    at_dp = lax.axis_index("dp")
    place = jnp.stack([at_dp >> (NY.bit_length() - 1), at_dp & (NY - 1)]).astype(jnp.int32)
    first, onehot, rank = tables(
        ids_t, route_weights.T, grad_out, flight, capacity, chunks[0][1]
    )
    rows = [first] + [
        pick(onehot, grad_out, start, width) for start, (_, width) in zip(starts[1:], chunks[1:])
    ]
    preact = saved_preact.reshape(slots, both)
    hidden = hidden_transposed(preact, rows[-1])

    def dispatch(part):
        width = part.shape[1]
        return lax.all_to_all(
            part.reshape(flight, capacity, width), "expert", split_axis=0, concat_axis=0, tiled=True
        ).reshape(slots, width)

    got = [dispatch(first)]
    scale = scale_row(got[0], starts[1])
    made = scale
    steps, arrived, number, parts = {}, {}, [0] * len(chunks), {}
    for item in order:
        if item == "gather":
            weight = lax.all_gather(hold(weight, made), "dp", axis=0, axis_index_groups=ALONG_Y)
            continue
        if item == "act":
            pre_grad, route = act_side(got, starts, weight, preact, made)
            made = route
            continue
        axis, width = chunks[item]
        if number[item] == 0:
            steps[item] = ring(axis, place, hidden, scale, got[item], width)
            arrived[item] = []
        made, arrived[item] = steps[item](number[item], arrived[item], made)
        if number[item] == 0 and item + 1 < len(chunks):
            got.append(dispatch(hold(rows[item + 1], made)))
        number[item] += 1
        if arrived[item] is None:
            parts[item] = exchange(made, "y" if axis == "z" else "z")
    own = sum_parts([parts[k] for k in range(len(chunks))])
    every = lax.all_gather(route[0], "expert").reshape(flight, flight, capacity)
    back = lax.dynamic_index_in_dim(every, lax.axis_index("expert"), 1, keepdims=False)
    route_grad = combine(back, ids_t, rank).T
    return (route_grad, pre_grad.reshape(saved_preact.shape), own[None])


CHUNKS = (("z", 2048), ("z", 2048))
ORDER = (0, "gather", 0, 1, 0, 1, 0, 1, 0, 1, "act", 1)


def solution(mesh):
    return jax.shard_map(
        functools.partial(per_device, CHUNKS, ORDER),
        mesh=mesh,
        in_specs=(
            P(("dp", "expert"), None),
            P(("dp", "expert"), None),
            P(("dp", "expert"), None),
            P("expert", "dp", None, None, None),
            P("expert", "dp", None),
        ),
        out_specs=(
            P(("dp", "expert"), None),
            P("expert", "dp", None, None, None),
            P("expert", "dp", None),
        ),
        check_vma=False,
    )
```
